128 devices in a mesh: seq: 16 (over x, y), dp: 8 (over z, core).
Axes of the slice: x: 4, y: 4, z: 4, core: 2. Of those that a mesh axis runs over, the one named last changes fastest.
Arguments:
- layer_input: bfloat16 [8, 5120, 6144], P('dp', 'seq'), may hold values from -6 to 6
- queries: bfloat16 [8, 5120, 4096], P('dp', 'seq'), may hold values from -6 to 6
- key_vectors: bfloat16 [8, 5120, 4096], P('dp', 'seq'), may hold values from -6 to 6
- value_vectors: bfloat16 [8, 5120, 4096], P('dp', 'seq'), may hold values from -6 to 6
- grad_attended: bfloat16 [8, 5120, 4096], P('dp', 'seq'), may hold values from -6 to 6
- log_decay: float32 [8, 32, 5120], P('dp', None, 'seq'), may hold values from -2 to 0, as said below
- kept_blocks: int32 [128], replicated, may hold values from 0 to 4607, as said below
Outputs:
- attended: bfloat16 [8, 5120, 4096], P('dp', 'seq')
- grad_queries: bfloat16 [8, 5120, 4096], P('dp', 'seq')
- grad_keys: bfloat16 [8, 5120, 4096], P('dp', 'seq')
- grad_values: bfloat16 [8, 5120, 4096], P('dp', 'seq')
- grad_blocks: float32 [128, 128, 128], P(('seq', 'dp'))
The draws below stay inside these ranges and needn't reach their ends.
Inputs may be any that keep to these rules, and one draw needn't show every extreme that they name: `kept_blocks`: distinct block numbers of the 48 x 96 blocks, row block major. `log_decay`: negative.
All inputs are finite; a program needn't handle non-finite values.
Results may differ from the reference program's by a relative error of at most 0.025.
Values may be sent and summed in bfloat16 or wider, within the bound.
No kernel may reach another device: no remote copies, remote signals or barrier semaphores. Data moves between devices by JAX's collectives and lax.ppermute only.
A program may use at most 192 MiB of HBM per device.

```python
import math
import jax
import jax.numpy as jnp
from jax import lax

D = 6144
LOCAL_HEADS = 32
HEAD_DIM = 128
BLOCK = 128
TOK_DEV = 320
SEQUENCE_LENGTH = 5120
BATCH_SEQUENCES = 8
TOKENS = 40960
KEEP = 128
ROW_BLOCKS = 48
COL_BLOCKS = 96


def draw_log_decay(key, part):
    key = jax.random.fold_in(key, 7)
    random_subkeys = jax.random.split(key, 7)
    fast_share = 0.5
    is_fast = jax.random.uniform(random_subkeys[0], (BATCH_SEQUENCES, LOCAL_HEADS, 1)) < fast_share
    fast_rate = jnp.exp(jax.random.uniform(random_subkeys[1], (BATCH_SEQUENCES, LOCAL_HEADS, 1), minval=jnp.log(0.046), maxval=jnp.log(0.077)))
    slow_rate = jnp.exp(jax.random.uniform(random_subkeys[2], (BATCH_SEQUENCES, LOCAL_HEADS, 1), minval=jnp.log(0.05), maxval=jnp.log(0.5))) / SEQUENCE_LENGTH
    baseline_rate = jnp.where(is_fast, fast_rate, slow_rate)
    position_multiplier = jnp.exp(jax.random.uniform(random_subkeys[3], (BATCH_SEQUENCES, LOCAL_HEADS, SEQUENCE_LENGTH), minval=jnp.log(0.4), maxval=jnp.log(1.6)))
    block_multiplier = jnp.exp(jax.random.uniform(random_subkeys[4], (BATCH_SEQUENCES, LOCAL_HEADS, SEQUENCE_LENGTH // TOK_DEV), minval=jnp.log(0.5), maxval=jnp.log(2.0)))
    block_multiplier = jnp.repeat(block_multiplier, TOK_DEV, axis=2)
    spike_positions = jax.random.randint(random_subkeys[5], (BATCH_SEQUENCES, LOCAL_HEADS, 2, 1), 0, SEQUENCE_LENGTH)
    spike_depth = jnp.log(jax.random.uniform(random_subkeys[6], (BATCH_SEQUENCES, LOCAL_HEADS, 2, 1), minval=0.5, maxval=0.8))
    spike_locations = jnp.arange(SEQUENCE_LENGTH)[None, None, None, :]
    spike_events = jnp.sum(jnp.where(spike_locations == spike_positions, spike_depth, 0.0), axis=2)
    return (spike_events - baseline_rate * position_multiplier * block_multiplier).astype(jnp.float32)


def draw_kept_blocks(key, part):
    key = jax.random.fold_in(key, 11)
    total_blocks = ROW_BLOCKS * COL_BLOCKS
    inner = jax.random.permutation(key, total_blocks - 2)[:KEEP - 2] + 1
    ends = jnp.array([0, total_blocks - 1], jnp.int32)
    merged = jnp.concatenate([ends, inner.astype(jnp.int32)])
    order = jax.random.permutation(jax.random.fold_in(key, 1), KEEP)
    return merged[order]


def steps_of(key, dims, cuts, least, high):
    level, own = 1.0, jax.random.fold_in(key, 6)
    for position, blocks in cuts:
        draws = jnp.exp(jax.random.uniform(jax.random.fold_in(own, position), (blocks,), jnp.float32, least / len(cuts), high / len(cuts)))
        level = level * jnp.repeat(draws, dims[position] // blocks).reshape([-1 if axis == position else 1 for axis in range(len(dims))])
    return level


def normal_values(rng, dims, deviation, limit, cuts=(), kind=jnp.bfloat16):
    values = deviation * jax.random.normal(rng, dims, jnp.float32)
    if cuts:
        values = values * steps_of(rng, dims, cuts, -0.22, 0.18)
    return jnp.clip(values, -limit, limit).astype(kind)


def setup_inputs(seed: int = 0) -> dict:
    keys = jax.random.split(jax.random.key(seed), 8)
    layer_input = normal_values(keys[0], (BATCH_SEQUENCES, SEQUENCE_LENGTH, D), 1.0, 6.0, ((0, 8), (1, 16)))
    queries = normal_values(keys[1], (BATCH_SEQUENCES, SEQUENCE_LENGTH, LOCAL_HEADS * HEAD_DIM), 1.0, 6.0, ((0, 8), (1, 16)))
    key_vectors = normal_values(keys[2], (BATCH_SEQUENCES, SEQUENCE_LENGTH, LOCAL_HEADS * HEAD_DIM), 1.0, 6.0, ((0, 8), (1, 16)))
    value_vectors = normal_values(keys[3], (BATCH_SEQUENCES, SEQUENCE_LENGTH, LOCAL_HEADS * HEAD_DIM), 1.0, 6.0, ((0, 8), (1, 16)))
    grad_attended = normal_values(keys[4], (BATCH_SEQUENCES, SEQUENCE_LENGTH, LOCAL_HEADS * HEAD_DIM), 1.0, 6.0, ((0, 8), (1, 16)))
    log_decay = draw_log_decay(jax.random.fold_in(keys[7], 71), 0)
    kept_blocks = draw_kept_blocks(jax.random.fold_in(keys[7], 71), 0)
    return {"layer_input": layer_input, "queries": queries, "key_vectors": key_vectors, "value_vectors": value_vectors, "grad_attended": grad_attended, "log_decay": log_decay, "kept_blocks": kept_blocks}


def rounded(values):
    return lax.optimization_barrier(values.astype(jnp.bfloat16)).astype(jnp.float32)

def sequence_pass(inputs):
    queries, key_vectors, value_vectors, grad_attended, log_decay = inputs
    blocks = SEQUENCE_LENGTH // TOK_DEV
    block_shape = (blocks, TOK_DEV, LOCAL_HEADS, HEAD_DIM)
    query_rows = queries.reshape(block_shape).astype(jnp.float32)
    key_rows = key_vectors.reshape(block_shape).astype(jnp.float32)
    value_rows = value_vectors.reshape(block_shape).astype(jnp.float32)
    upstream = grad_attended.reshape(block_shape).astype(jnp.float32)
    cumulative = jnp.cumsum(log_decay.reshape(LOCAL_HEADS, blocks, TOK_DEV), axis=2).transpose(1, 0, 2)
    block_log = cumulative[:, :, -1]
    causal = jnp.tril(jnp.ones((TOK_DEV, TOK_DEV), dtype=bool))
    log_gaps = cumulative[:, :, :, None] - cumulative[:, :, None, :]
    within = jnp.where(causal, jnp.exp(jnp.minimum(log_gaps, 0.0)), 0.0)
    scores = jnp.einsum('bthc,bshc->bhts', query_rows, key_rows)
    weights = rounded(scores * within)
    tail_decay = jnp.exp(block_log[:, :, None] - cumulative).transpose(0, 2, 1)[..., None]
    head_decay = jnp.exp(cumulative).transpose(0, 2, 1)[..., None]
    scaled_keys = rounded(tail_decay * key_rows)
    scaled_queries = rounded(head_decay * query_rows)
    block_state = rounded(jnp.einsum('bshc,bshe->bhce', scaled_keys, value_rows))
    initial = jnp.zeros((LOCAL_HEADS, HEAD_DIM, HEAD_DIM), jnp.float32)

    def forward_step(running, element):
        state_here, log_here = element
        return (jnp.exp(log_here)[:, None, None] * running + state_here, running)
    _, carried = lax.scan(forward_step, initial, (block_state, block_log))
    carried = rounded(carried)
    raw_output = jnp.einsum('bhts,bshe->bthe', weights, value_rows) + jnp.einsum('bthc,bhce->bthe', scaled_queries, carried)
    inverse = lax.rsqrt(lax.optimization_barrier(jnp.mean(raw_output * raw_output, axis=3, keepdims=True)) + 1e-06)
    normed = raw_output * inverse
    grad_raw = rounded(inverse * (upstream - normed * lax.optimization_barrier(jnp.mean(upstream * normed, axis=3, keepdims=True))))
    block_grad = rounded(jnp.einsum('bthc,bthe->bhce', scaled_queries, grad_raw))
    _, later_grad = lax.scan(forward_step, initial, (block_grad, block_log), reverse=True)
    later_grad = rounded(later_grad)
    dscores = rounded(jnp.einsum('bthe,bshe->bhts', grad_raw, value_rows) * within)
    grad_q = jnp.einsum('bhts,bshc->bthc', dscores, key_rows) + head_decay * jnp.einsum('bthe,bhce->bthc', grad_raw, carried)
    grad_k = jnp.einsum('bhts,bthc->bshc', dscores, query_rows) + tail_decay * jnp.einsum('bshe,bhce->bshc', value_rows, later_grad)
    grad_v = jnp.einsum('bhts,bthe->bshe', weights, grad_raw) + jnp.einsum('bshc,bhce->bshe', scaled_keys, later_grad)
    flat = (SEQUENCE_LENGTH, LOCAL_HEADS * HEAD_DIM)
    return (normed.astype(jnp.bfloat16).reshape(flat), grad_q.astype(jnp.bfloat16).reshape(flat), grad_k.astype(jnp.bfloat16).reshape(flat), grad_v.astype(jnp.bfloat16).reshape(flat))

def reference(layer_input, queries, key_vectors, value_vectors, grad_attended, log_decay, kept_blocks):
    attended, grad_queries, grad_keys, grad_values = lax.map(sequence_pass, (queries, key_vectors, value_vectors, grad_attended, log_decay))
    stacked = jnp.concatenate([grad_queries, grad_keys, grad_values], axis=2).reshape(TOKENS, 3 * LOCAL_HEADS * HEAD_DIM)
    flat_input = layer_input.reshape(TOKENS, D)

    def one_block(block_id):
        row_start = (block_id // COL_BLOCKS * BLOCK).astype(jnp.int32)
        col_start = (block_id % COL_BLOCKS * BLOCK).astype(jnp.int32)
        input_cols = lax.dynamic_slice_in_dim(flat_input, row_start, BLOCK, 1)
        grad_cols = lax.dynamic_slice_in_dim(stacked, col_start, BLOCK, 1)
        return jnp.dot(input_cols.T, grad_cols, preferred_element_type=jnp.float32)
    grad_blocks = lax.map(one_block, kept_blocks) * (1.0 / math.sqrt(TOKENS))
    return (attended, grad_queries, grad_keys, grad_values, grad_blocks)
```

```python
import functools
import math

import jax
import jax.numpy as jnp
from jax import lax
from jax.experimental import pallas as pl
from jax.experimental.pallas import tpu as pltpu
from jax.sharding import Mesh
from jax.sharding import PartitionSpec as P

BLOCK = 128
GROUP = 8
AUX = 16
F32 = jnp.float32
BF16 = jnp.bfloat16
MIB = 1 << 20


def dot_nt(a, b):
    return lax.dot_general(a, b, (((1,), (1,)), ((), ())), preferred_element_type=F32)


def dot_nn(a, b):
    return lax.dot_general(a, b, (((1,), (0,)), ((), ())), preferred_element_type=F32)


def dot_tn(a, b):
    return lax.dot_general(a, b, (((0,), (0,)), ((), ())), preferred_element_type=F32)


def head_slice(h):
    return slice(h * BLOCK, (h + 1) * BLOCK)


def row_cuts(length):
    return [(r, min(r + BLOCK, length)) for r in range(0, length, BLOCK)]


def states_kernel(decay_ref, k_ref, v_ref, payload_ref, col_ref, row_ref):
    length = k_ref.shape[1]
    decay = decay_ref[0]
    high = decay.astype(BF16).astype(F32)
    rest = decay - high
    middle = rest.astype(BF16).astype(F32)
    terms = jnp.concatenate([high, middle, rest - middle], axis=0).astype(BF16)
    t = lax.broadcasted_iota(jnp.int32, (length, length), 0)
    s = lax.broadcasted_iota(jnp.int32, (length, length), 1)
    lower = jnp.where(s <= t, 1.0, 0.0).astype(BF16)
    upper = jnp.where(t <= s, 1.0, 0.0).astype(BF16)
    cols = dot_nt(lower, terms)
    col = cols[:, :GROUP] + cols[:, GROUP : 2 * GROUP] + cols[:, 2 * GROUP :]
    rows = dot_nn(terms, upper)
    row = rows[:GROUP] + rows[GROUP : 2 * GROUP] + rows[2 * GROUP :]
    col_ref[0] = col
    row_ref[0] = row
    total = col[length - 1 : length, :]
    tail = jnp.exp(total - col)
    whole = jnp.exp(total)
    index = lax.broadcasted_iota(jnp.int32, (AUX, BLOCK), 0)
    for h in range(GROUP):
        keys = k_ref[0, :, head_slice(h)].astype(F32)
        scaled = (keys * tail[:, h : h + 1]).astype(BF16)
        state = dot_tn(scaled, v_ref[0, :, head_slice(h)])
        payload_ref[h // 2, head_slice(h % 2), :] = state.astype(BF16)
    for p in range(GROUP // 2):
        aux = jnp.zeros((AUX, BLOCK), F32)
        for i in range(2):
            value = jnp.broadcast_to(whole[:, 2 * p + i : 2 * p + i + 1], (AUX, BLOCK))
            first = value.astype(BF16).astype(F32)
            aux = jnp.where(index == 2 * i, first, aux)
            aux = jnp.where(index == 2 * i + 1, value - first, aux)
        payload_ref[p, 2 * BLOCK :, :] = aux.astype(BF16)


def scan_kernel(reverse, x_ref, aux_ref, out_ref):
    blocks = x_ref.shape[0]
    running = [jnp.zeros((BLOCK, BLOCK), F32) for _ in range(2)]
    for step in range(blocks):
        j = blocks - 1 - step if reverse else step
        aux = aux_ref[j].astype(F32)
        for i in range(2):
            out_ref[j, head_slice(i), :] = running[i].astype(BF16)
            whole = aux[2 * i : 2 * i + 1] + aux[2 * i + 1 : 2 * i + 2]
            running[i] = running[i] * whole + x_ref[j, head_slice(i), :].astype(F32)


def intra_kernel(q_ref, k_ref, v_ref, col_ref, row_ref, raw_ref):
    length = q_ref.shape[1]
    col = col_ref[0]
    for h in range(GROUP):
        sl = head_slice(h)
        for r0, r1 in row_cuts(length):
            scores = dot_nt(q_ref[0, r0:r1, sl], k_ref[0, :r1, sl])
            within = jnp.exp(col[r0:r1, h : h + 1] - row_ref[0, h : h + 1, :r1])
            t = lax.broadcasted_iota(jnp.int32, (r1 - r0, r1), 0) + r0
            s = lax.broadcasted_iota(jnp.int32, (r1 - r0, r1), 1)
            weights = (scores * jnp.where(s <= t, within, 0.0)).astype(BF16)
            raw_ref[0, r0:r1, sl] = dot_nn(weights, v_ref[0, :r1, sl])


def norm_kernel(raw_ref, q_ref, g_ref, col_ref, carried_ref, attended_ref, grad_raw_ref, grad_ref):
    head_decay = jnp.exp(col_ref[0])
    for h in range(GROUP):
        sl = head_slice(h)
        scaled = (q_ref[0, :, sl].astype(F32) * head_decay[:, h : h + 1]).astype(BF16)
        raw = raw_ref[0, :, sl] + dot_nn(scaled, carried_ref[h])
        inverse = lax.rsqrt(jnp.mean(raw * raw, axis=1, keepdims=True) + 1e-6)
        normed = raw * inverse
        upstream = g_ref[0, :, sl].astype(F32)
        shared = jnp.mean(upstream * normed, axis=1, keepdims=True)
        grad_raw = (inverse * (upstream - normed * shared)).astype(BF16)
        attended_ref[0, :, sl] = normed.astype(BF16)
        grad_raw_ref[0, :, sl] = grad_raw
        grad_ref[h] = dot_tn(scaled, grad_raw).astype(BF16)


def grad_q_kernel(
    grad_raw_ref, k_ref, v_ref, col_ref, row_ref, carried_ref, grad_q_ref, by_head_ref
):
    length = k_ref.shape[1]
    col = col_ref[0]
    head_decay = jnp.exp(col)
    for h in range(GROUP):
        sl = head_slice(h)
        for r0, r1 in row_cuts(length):
            grad_raw = grad_raw_ref[0, r0:r1, sl]
            scores = dot_nt(grad_raw, v_ref[0, :r1, sl])
            within = jnp.exp(col[r0:r1, h : h + 1] - row_ref[0, h : h + 1, :r1])
            t = lax.broadcasted_iota(jnp.int32, (r1 - r0, r1), 0) + r0
            s = lax.broadcasted_iota(jnp.int32, (r1 - r0, r1), 1)
            dscores = (scores * jnp.where(s <= t, within, 0.0)).astype(BF16)
            grad_q = dot_nn(dscores, k_ref[0, :r1, sl])
            grad_q = grad_q + head_decay[r0:r1, h : h + 1] * dot_nt(grad_raw, carried_ref[h])
            grad_q = grad_q.astype(BF16)
            grad_q_ref[0, r0:r1, sl] = grad_q
            by_head_ref[h, r0:r1, :] = grad_q


def grad_kv_kernel(
    grad_raw_ref, q_ref, k_ref, v_ref, col_ref, row_ref, grad_k_ref, grad_v_ref
):
    length = k_ref.shape[1]
    col = col_ref[0]
    for h in range(GROUP):
        sl = head_slice(h)
        for s0, s1 in row_cuts(length):
            queries = q_ref[0, s0:, sl]
            grad_raw = grad_raw_ref[0, s0:, sl]
            within = jnp.exp(row_ref[0, h : h + 1, s0:] - col[s0:s1, h : h + 1])
            s = lax.broadcasted_iota(jnp.int32, (s1 - s0, length - s0), 0)
            t = lax.broadcasted_iota(jnp.int32, (s1 - s0, length - s0), 1)
            within = jnp.where(s <= t, within, 0.0)
            weights = (dot_nt(k_ref[0, s0:s1, sl], queries) * within).astype(BF16)
            dscores = (dot_nt(v_ref[0, s0:s1, sl], grad_raw) * within).astype(BF16)
            grad_k_ref[0, s0:s1, sl] = dot_nn(dscores, queries)
            grad_v_ref[0, s0:s1, sl] = dot_nn(weights, grad_raw)


def kept_kernel(
    heads,
    kept_ref,
    core_ref,
    k_ref,
    v_ref,
    intra_k_ref,
    intra_v_ref,
    col_ref,
    later_ref,
    by_head_ref,
    turned_ref,
    grad_k_ref,
    grad_v_ref,
    theirs_ref,
    mine_ref,
    stack,
    turned,
    stack_sem,
    turned_sem,
):
    length = k_ref.shape[1]
    group = pl.program_id(0)
    copies = (
        pltpu.make_async_copy(by_head_ref, stack.at[pl.ds(0, heads)], stack_sem),
        pltpu.make_async_copy(turned_ref, turned, turned_sem),
    )

    @pl.when(group == 0)
    def _():
        for copy in copies:
            copy.start()

    col = col_ref[0]
    tail = jnp.exp(col[length - 1 : length, :] - col)
    for h in range(GROUP):
        sl = head_slice(h)
        later = later_ref[h]
        factor = tail[:, h : h + 1]
        scaled = (k_ref[0, :, sl].astype(F32) * factor).astype(BF16)
        grad_k = intra_k_ref[0, :, sl] + factor * dot_nt(v_ref[0, :, sl], later)
        grad_v = intra_v_ref[0, :, sl] + dot_nn(scaled, later)
        grad_k = grad_k.astype(BF16)
        grad_v = grad_v.astype(BF16)
        grad_k_ref[0, :, sl] = grad_k
        grad_v_ref[0, :, sl] = grad_v
        stack[heads + group * GROUP + h] = grad_k
        stack[2 * heads + group * GROUP + h] = grad_v

    @pl.when(group == pl.num_programs(0) - 1)
    def _():
        for copy in copies:
            copy.wait()
        core = core_ref[0]
        per_row = 3 * heads

        def run(out_ref, parity):
            def body(i, carry):
                number = kept_ref[2 * i + parity]
                left = turned[number // per_row]
                right = stack[lax.rem(number, per_row)]
                out_ref[i] = dot_nn(left, right).astype(BF16)
                return carry

            lax.fori_loop(0, out_ref.shape[0], body, 0, unroll=4)

        run(theirs_ref, 1 - core)
        run(mine_ref, core)


def params(mib):
    return pltpu.CompilerParams(
        dimension_semantics=("arbitrary",), vmem_limit_bytes=mib * MIB
    )


def cost(flops, bytes_accessed, transcendentals=0):
    return pl.CostEstimate(
        flops=flops, bytes_accessed=bytes_accessed, transcendentals=transcendentals
    )


def per_device(
    layer_input, queries, key_vectors, value_vectors, grad_attended, log_decay, kept_blocks
):
    heads = log_decay.shape[1]
    length = queries.shape[1]
    width = queries.shape[2]
    groups = heads // GROUP
    wide = GROUP * BLOCK
    kept = kept_blocks.shape[0]
    seq = ("x", "y")
    blocks = lax.axis_size(seq)
    per_owner = heads // blocks
    rows = per_owner * BLOCK
    pair = GROUP // per_owner

    tokens = pl.BlockSpec((1, length, wide), lambda g, *_: (0, 0, g))
    col_spec = pl.BlockSpec((1, length, GROUP), lambda g, *_: (g, 0, 0))
    row_spec = pl.BlockSpec((1, GROUP, length), lambda g, *_: (g, 0, 0))
    square = pl.BlockSpec((GROUP, BLOCK, BLOCK), lambda g, *_: (g, 0, 0))
    by_head = pl.BlockSpec((GROUP, length, BLOCK), lambda g, *_: (g, 0, 0))
    flat_bf = jax.ShapeDtypeStruct((1, length, width), BF16)
    flat_f32 = jax.ShapeDtypeStruct((1, length, width), F32)
    squares = jax.ShapeDtypeStruct((heads, BLOCK, BLOCK), BF16)
    whole = pl.BlockSpec(memory_space=pltpu.VMEM)
    pairs = heads * length * length

    decay = log_decay[0].reshape(groups, GROUP, length)
    payload, col, row = pl.pallas_call(
        states_kernel,
        grid=(groups,),
        in_specs=[row_spec, tokens, tokens],
        out_specs=[
            pl.BlockSpec((pair, rows + AUX, BLOCK), lambda g: (g, 0, 0)),
            col_spec,
            row_spec,
        ],
        out_shape=[
            jax.ShapeDtypeStruct((blocks, rows + AUX, BLOCK), BF16),
            jax.ShapeDtypeStruct((groups, length, GROUP), F32),
            jax.ShapeDtypeStruct((groups, GROUP, length), F32),
        ],
        compiler_params=params(16),
        name="states",
    )(decay, key_vectors, value_vectors)

    received = lax.all_to_all(payload, seq, 0, 0, tiled=True)

    intra = pl.pallas_call(
        intra_kernel,
        grid=(groups,),
        in_specs=[tokens, tokens, tokens, col_spec, row_spec],
        out_specs=tokens,
        out_shape=flat_f32,
        compiler_params=params(16),
        cost_estimate=cost(pairs * 4 * BLOCK, 6 * length * width * 2, pairs),
        name="intra",
    )(queries, key_vectors, value_vectors, col, row)

    turned = layer_input[0].reshape(length, -1, BLOCK).transpose(1, 2, 0)

    aux = received[:, rows:, :]

    def scan(x, reverse):
        return pl.pallas_call(
            functools.partial(scan_kernel, reverse),
            in_specs=[whole, whole],
            out_specs=whole,
            out_shape=jax.ShapeDtypeStruct((blocks, rows, BLOCK), BF16),
            compiler_params=pltpu.CompilerParams(vmem_limit_bytes=8 * MIB),
            name="scan",
        )(x, aux)

    carried = lax.all_to_all(scan(received, False), seq, 0, 0, tiled=True)
    carried = carried.reshape(heads, BLOCK, BLOCK)

    attended, grad_raw, block_grad = pl.pallas_call(
        norm_kernel,
        grid=(groups,),
        in_specs=[tokens, tokens, tokens, col_spec, square],
        out_specs=[tokens, tokens, square],
        out_shape=[flat_bf, flat_bf, squares],
        compiler_params=params(20),
        name="norm",
    )(intra, queries, grad_attended, col, carried)

    sent = lax.all_to_all(block_grad.reshape(blocks, rows, BLOCK), seq, 0, 0, tiled=True)

    grad_q, grad_q_by_head = pl.pallas_call(
        grad_q_kernel,
        grid=(groups,),
        in_specs=[tokens, tokens, tokens, col_spec, row_spec, square],
        out_specs=[tokens, by_head],
        out_shape=[flat_bf, jax.ShapeDtypeStruct((heads, length, BLOCK), BF16)],
        compiler_params=params(16),
        cost_estimate=cost(pairs * 4 * BLOCK, 6 * length * width * 2, pairs),
        name="grad_q",
    )(grad_raw, key_vectors, value_vectors, col, row, carried)

    later = lax.all_to_all(scan(sent, True), seq, 0, 0, tiled=True)
    later = later.reshape(heads, BLOCK, BLOCK)

    intra_k, intra_v = pl.pallas_call(
        grad_kv_kernel,
        grid=(groups,),
        in_specs=[tokens, tokens, tokens, tokens, col_spec, row_spec],
        out_specs=[tokens, tokens],
        out_shape=[flat_f32, flat_f32],
        compiler_params=params(20),
        cost_estimate=cost(pairs * 8 * BLOCK, 8 * length * width * 2, pairs),
        name="grad_kv",
    )(grad_raw, queries, key_vectors, value_vectors, col, row)

    core = lax.axis_index("core").astype(jnp.int32).reshape(1)
    half = jax.ShapeDtypeStruct((kept // 2, BLOCK, BLOCK), BF16)
    half_spec = pl.BlockSpec((kept // 2, BLOCK, BLOCK), lambda g, *_: (0, 0, 0))
    hbm = pl.BlockSpec(memory_space=pl.ANY)
    grad_k, grad_v, theirs, mine = pl.pallas_call(
        functools.partial(kept_kernel, heads),
        grid_spec=pltpu.PrefetchScalarGridSpec(
            num_scalar_prefetch=2,
            grid=(groups,),
            in_specs=[tokens, tokens, tokens, tokens, col_spec, square, hbm, hbm],
            out_specs=[tokens, tokens, half_spec, half_spec],
            scratch_shapes=[
                pltpu.VMEM((3 * heads, length, BLOCK), BF16),
                pltpu.VMEM(turned.shape, BF16),
                pltpu.SemaphoreType.DMA,
                pltpu.SemaphoreType.DMA,
            ],
        ),
        out_shape=[flat_bf, flat_bf, half, half],
        compiler_params=params(44),
        name="kept",
    )(
        kept_blocks,
        core,
        key_vectors,
        value_vectors,
        intra_k,
        intra_v,
        col,
        later,
        grad_q_by_head,
        turned,
    )

    other = lax.ppermute(theirs, "core", [(0, 1), (1, 0)])
    chip = (mine.astype(F32) + other.astype(F32)).astype(BF16)
    parts = lax.all_to_all(chip, ("x", "y", "z"), 0, 0, tiled=True)
    tokens_all = length * lax.axis_size(("x", "y", "z", "core"))
    grad_blocks = jnp.sum(parts.astype(F32), axis=0, keepdims=True) / math.sqrt(tokens_all)
    return attended, grad_q, grad_k, grad_v, grad_blocks


def solution(mesh):
    physical = Mesh(mesh.devices.reshape(4, 4, 4, 2), ("x", "y", "z", "core"))
    seq, dp = ("x", "y"), ("z", "core")
    tokens = P(dp, seq, None)
    return jax.shard_map(
        per_device,
        mesh=physical,
        in_specs=(tokens, tokens, tokens, tokens, tokens, P(dp, None, seq), P()),
        out_specs=(tokens, tokens, tokens, tokens, P(seq + dp, None, None)),
        check_vma=False,
    )
```

```python
import functools
import math

import jax
import jax.numpy as jnp
from jax import lax
from jax.experimental import pallas as pl
from jax.experimental.pallas import tpu as pltpu
from jax.sharding import Mesh
from jax.sharding import PartitionSpec as P

BLOCK = 128
GROUP = 8
WIDE = 256
KEPT_UNROLL = 16
AUX = 16
F32 = jnp.float32
BF16 = jnp.bfloat16
MIB = 1 << 20


def dot_nt(a, b):
    return lax.dot_general(a, b, (((1,), (1,)), ((), ())), preferred_element_type=F32)


def dot_nn(a, b):
    return lax.dot_general(a, b, (((1,), (0,)), ((), ())), preferred_element_type=F32)


def dot_tn(a, b):
    return lax.dot_general(a, b, (((0,), (0,)), ((), ())), preferred_element_type=F32)


def head_slice(h):
    return slice(h * BLOCK, (h + 1) * BLOCK)


def batches(size):
    return [range(h, h + size) for h in range(0, GROUP, size)]


def states_kernel(decay_ref, k_ref, v_ref, payload_ref, col_ref, row_ref):
    length = k_ref.shape[1]
    group = pl.program_id(0)
    groups = col_ref.shape[0]
    heads = groups * GROUP

    @pl.when(group == 0)
    def _():
        decay = decay_ref[...]
        high = decay.astype(BF16).astype(F32)
        rest = decay - high
        middle = rest.astype(BF16).astype(F32)
        terms = jnp.concatenate([high, middle, rest - middle], axis=0).astype(BF16)
        t = lax.broadcasted_iota(jnp.int32, (length, length), 0)
        s = lax.broadcasted_iota(jnp.int32, (length, length), 1)
        lower = jnp.where(s <= t, 1.0, 0.0).astype(BF16)
        upper = jnp.where(t <= s, 1.0, 0.0).astype(BF16)
        cols = dot_nt(lower, terms)
        rows = dot_nn(terms, upper)
        row = rows[:heads] + rows[heads : 2 * heads] + rows[2 * heads :]
        for g in range(groups):
            at = [slice(n * heads + g * GROUP, n * heads + (g + 1) * GROUP) for n in range(3)]
            col_ref[g] = cols[:, at[0]] + cols[:, at[1]] + cols[:, at[2]]
            row_ref[g] = row[g * GROUP : (g + 1) * GROUP]

    col = col_ref[group]
    total = col[length - 1 : length, :]
    tail = jnp.exp(total - col)
    whole = jnp.exp(total)
    index = lax.broadcasted_iota(jnp.int32, (AUX, BLOCK), 0)
    for hs in batches(4):
        scaled = [v_ref[0, :, head_slice(h)].astype(F32) * tail[:, h : h + 1] for h in hs]
        states = [dot_tn(k_ref[0, :, head_slice(h)], x.astype(BF16)) for h, x in zip(hs, scaled)]
        for h, state in zip(hs, states):
            payload_ref[h // 2, head_slice(h % 2), :] = state.astype(BF16)
    for p in range(GROUP // 2):
        aux = jnp.zeros((AUX, BLOCK), F32)
        for i in range(2):
            value = jnp.broadcast_to(whole[:, 2 * p + i : 2 * p + i + 1], (AUX, BLOCK))
            first = value.astype(BF16).astype(F32)
            aux = jnp.where(index == 2 * i, first, aux)
            aux = jnp.where(index == 2 * i + 1, value - first, aux)
        payload_ref[p, 2 * BLOCK :, :] = aux.astype(BF16)


def first_scan_kernel(x_ref, after_ref, out_ref, whole_ref):
    del after_ref
    blocks = x_ref.shape[0]
    running = [jnp.zeros((BLOCK, BLOCK), F32) for _ in range(2)]
    for j in range(blocks):
        aux = x_ref[j, 2 * BLOCK :, :].astype(F32)
        for i in range(2):
            out_ref[j, head_slice(i), :] = running[i].astype(BF16)
            whole = aux[2 * i : 2 * i + 1] + aux[2 * i + 1 : 2 * i + 2]
            whole_ref[j, i : i + 1, :] = whole
            running[i] = running[i] * whole + x_ref[j, head_slice(i), :].astype(F32)


def second_scan_kernel(x_ref, whole_ref, after_ref, out_ref):
    del after_ref
    blocks = x_ref.shape[0]
    running = [jnp.zeros((BLOCK, BLOCK), F32) for _ in range(2)]
    for j in range(blocks - 1, -1, -1):
        for i in range(2):
            out_ref[j, head_slice(i), :] = running[i].astype(BF16)
            whole = whole_ref[j, i : i + 1, :]
            running[i] = running[i] * whole + x_ref[j, head_slice(i), :].astype(F32)


def within(gap, offset):
    t = lax.broadcasted_iota(jnp.int32, gap.shape, 0)
    s = lax.broadcasted_iota(jnp.int32, gap.shape, 1) + offset
    return jnp.where(s <= t, jnp.exp(gap), 0.0)


def intra_kernel(q_ref, k_ref, v_ref, col_ref, row_ref, raw_ref, scaled_ref):
    col = col_ref[0]
    head_decay = jnp.exp(col)
    for hs in batches(2):
        parts = []
        for h in hs:
            sl = head_slice(h)
            at = slice(h, h + 1)
            scores = dot_nt(q_ref[0, :, sl], k_ref[0, :WIDE, sl])
            weights = scores * within(col[:, at] - row_ref[0, at, :WIDE], 0)
            scores = dot_nt(q_ref[0, WIDE:, sl], k_ref[0, WIDE:, sl])
            gap = col[WIDE:, at] - row_ref[0, at, WIDE:]
            parts.append((weights.astype(BF16), (scores * within(gap, 0)).astype(BF16)))
        for h, (weights, last) in zip(hs, parts):
            sl = head_slice(h)
            raw = dot_nn(weights, v_ref[0, :WIDE, sl])
            end = raw[WIDE:] + dot_nn(last, v_ref[0, WIDE:, sl])
            raw_ref[0, :WIDE, sl] = raw[:WIDE]
            raw_ref[0, WIDE:, sl] = end
            queries = q_ref[0, :, sl].astype(F32)
            scaled_ref[0, :, sl] = (queries * head_decay[:, h : h + 1]).astype(BF16)


def turn_kernel(x_ref, out_ref):
    for n in range(out_ref.shape[0]):
        out_ref[n] = x_ref[0, :, head_slice(n)].T


def norm_kernel(
    raw_ref, scaled_ref, g_ref, carried_ref, attended_ref, grad_raw_ref, grad_ref
):
    for hs in batches(8):
        sls = [head_slice(h) for h in hs]
        raws = [dot_nn(scaled_ref[0, :, sl], carried_ref[h]) for h, sl in zip(hs, sls)]
        raws = [raw + raw_ref[0, :, sl] for raw, sl in zip(raws, sls)]
        squares = [jnp.mean(raw * raw, axis=1, keepdims=True) for raw in raws]
        shareds = [
            jnp.mean(g_ref[0, :, sl].astype(F32) * raw, axis=1, keepdims=True)
            for raw, sl in zip(raws, sls)
        ]
        inverses = [lax.rsqrt(square + 1e-6) for square in squares]
        grads = []
        for raw, inverse, shared, sl in zip(raws, inverses, shareds, sls):
            normed = raw * inverse
            attended_ref[0, :, sl] = normed.astype(BF16)
            upstream = g_ref[0, :, sl].astype(F32)
            grad_raw = (inverse * (upstream - normed * (shared * inverse))).astype(BF16)
            grad_raw_ref[0, :, sl] = grad_raw
            grads.append(grad_raw)
        for h, sl, grad_raw in zip(hs, sls, grads):
            grad_ref[h] = dot_tn(scaled_ref[0, :, sl], grad_raw).astype(BF16)


def grad_q_kernel(
    grad_raw_ref,
    k_ref,
    v_ref,
    col_ref,
    row_ref,
    carried_ref,
    grad_q_ref,
    by_head_ref,
):
    col = col_ref[0]
    head_decay = jnp.exp(col)
    for hs in batches(2):
        parts = []
        for h in hs:
            sl = head_slice(h)
            at = slice(h, h + 1)
            scores = dot_nt(grad_raw_ref[0, :, sl], v_ref[0, :WIDE, sl])
            dscores = scores * within(col[:, at] - row_ref[0, at, :WIDE], 0)
            scores = dot_nt(grad_raw_ref[0, WIDE:, sl], v_ref[0, WIDE:, sl])
            gap = col[WIDE:, at] - row_ref[0, at, WIDE:]
            parts.append((dscores.astype(BF16), (scores * within(gap, 0)).astype(BF16)))
        for h, (dscores, last) in zip(hs, parts):
            sl = head_slice(h)
            carried = dot_nt(grad_raw_ref[0, :, sl], carried_ref[h])
            grad_q = dot_nn(dscores, k_ref[0, :WIDE, sl]) + head_decay[:, h : h + 1] * carried
            end = grad_q[WIDE:] + dot_nn(last, k_ref[0, WIDE:, sl])
            for cut, part in ((slice(0, WIDE), grad_q[:WIDE]), (slice(WIDE, None), end)):
                part = part.astype(BF16)
                grad_q_ref[0, cut, sl] = part
                by_head_ref[h, cut, :] = part


def grad_kv_kernel(
    grad_raw_ref,
    q_ref,
    k_ref,
    v_ref,
    col_ref,
    row_ref,
    grad_k_ref,
    grad_v_ref,
    scaled_k_ref,
    scaled_v_ref,
):
    length = k_ref.shape[1]
    col = col_ref[0]
    tail = jnp.exp(col[length - 1 : length, :] - col)
    split = length - WIDE

    def turned_within(h, rows, start, stop):
        gap = row_ref[0, h : h + 1, start:stop] - col[:rows, h : h + 1]
        s = lax.broadcasted_iota(jnp.int32, gap.shape, 0)
        t = lax.broadcasted_iota(jnp.int32, gap.shape, 1) + start
        return jnp.where(s <= t, jnp.exp(gap), 0.0)

    for hs in batches(2):
        parts = []
        for h in hs:
            sl = head_slice(h)
            near = turned_within(h, length, split, length)
            first = turned_within(h, split, 0, split)
            parts.append(
                [
                    (dot_nt(k_ref[0, :, sl], q_ref[0, split:, sl]) * near).astype(BF16),
                    (dot_nt(v_ref[0, :, sl], grad_raw_ref[0, split:, sl]) * near).astype(BF16),
                    (dot_nt(k_ref[0, :split, sl], q_ref[0, :split, sl]) * first).astype(BF16),
                    (dot_nt(v_ref[0, :split, sl], grad_raw_ref[0, :split, sl]) * first).astype(BF16),
                ]
            )
        for h, (weights, dscores, first_weights, first_dscores) in zip(hs, parts):
            sl = head_slice(h)
            grad_k = dot_nn(dscores, q_ref[0, split:, sl])
            grad_v = dot_nn(weights, grad_raw_ref[0, split:, sl])
            first_k = grad_k[:split] + dot_nn(first_dscores, q_ref[0, :split, sl])
            first_v = grad_v[:split] + dot_nn(first_weights, grad_raw_ref[0, :split, sl])
            grad_k_ref[0, :split, sl] = first_k.astype(BF16)
            grad_k_ref[0, split:, sl] = grad_k[split:].astype(BF16)
            grad_v_ref[0, :split, sl] = first_v.astype(BF16)
            grad_v_ref[0, split:, sl] = grad_v[split:].astype(BF16)
            factor = tail[:, h : h + 1]
            scaled_k_ref[0, :, sl] = (k_ref[0, :, sl].astype(F32) * factor).astype(BF16)
            scaled_v_ref[0, :, sl] = (v_ref[0, :, sl].astype(F32) * factor).astype(BF16)


def kept_kernel(
    heads,
    kept_ref,
    core_ref,
    scaled_k_ref,
    scaled_v_ref,
    intra_k_ref,
    intra_v_ref,
    later_ref,
    by_head_ref,
    turned_ref,
    grad_k_ref,
    grad_v_ref,
    theirs_ref,
    mine_ref,
    stack,
    turned,
    stack_sem,
    turned_sem,
):
    group = pl.program_id(0)
    copies = (
        pltpu.make_async_copy(by_head_ref, stack.at[pl.ds(0, heads)], stack_sem),
        pltpu.make_async_copy(turned_ref, turned, turned_sem),
    )

    @pl.when(group == 0)
    def _():
        for copy in copies:
            copy.start()

    for hs in batches(4):
        sls = [head_slice(h) for h in hs]
        grads_k = [dot_nt(scaled_v_ref[0, :, sl], later_ref[h]) for h, sl in zip(hs, sls)]
        grads_v = [dot_nn(scaled_k_ref[0, :, sl], later_ref[h]) for h, sl in zip(hs, sls)]
        for h, sl, grad_k, grad_v in zip(hs, sls, grads_k, grads_v):
            grad_k = (intra_k_ref[0, :, sl].astype(F32) + grad_k).astype(BF16)
            grad_v = (intra_v_ref[0, :, sl].astype(F32) + grad_v).astype(BF16)
            grad_k_ref[0, :, sl] = grad_k
            grad_v_ref[0, :, sl] = grad_v
            stack[heads + group * GROUP + h] = grad_k
            stack[2 * heads + group * GROUP + h] = grad_v

    @pl.when(group == pl.num_programs(0) - 1)
    def _():
        for copy in copies:
            copy.wait()
        core = core_ref[0]
        per_row = 3 * heads

        def run(out_ref, parity):
            def body(i, carry):
                number = kept_ref[2 * i + parity]
                left = turned[number // per_row]
                right = stack[lax.rem(number, per_row)]
                out_ref[i] = dot_nn(left, right).astype(BF16)
                return carry

            lax.fori_loop(0, out_ref.shape[0], body, 0, unroll=KEPT_UNROLL)

        run(theirs_ref, 1 - core)
        run(mine_ref, core)


def in_hbm(x):
    return pltpu.with_memory_space_constraint(x, pltpu.HBM)


def in_vmem(x):
    return pltpu.with_memory_space_constraint(x, pltpu.VMEM)


def call(name, kernel, grid, in_specs, out_specs, out_shape, mib, work=None, prefetch=0, scratch=()):
    estimate = None
    if work is not None:
        estimate = pl.CostEstimate(flops=work[0], bytes_accessed=work[1], transcendentals=0)
    return pl.pallas_call(
        kernel,
        grid_spec=pltpu.PrefetchScalarGridSpec(
            num_scalar_prefetch=prefetch,
            grid=grid,
            in_specs=in_specs,
            out_specs=out_specs,
            scratch_shapes=scratch,
        ),
        out_shape=out_shape,
        compiler_params=pltpu.CompilerParams(
            dimension_semantics=("arbitrary",) * len(grid), vmem_limit_bytes=mib * MIB
        ),
        cost_estimate=estimate,
        name=name,
    )


def per_device(
    layer_input, queries, key_vectors, value_vectors, grad_attended, log_decay, kept_blocks
):
    heads = log_decay.shape[1]
    length = queries.shape[1]
    width = queries.shape[2]
    groups = heads // GROUP
    wide = GROUP * BLOCK
    kept = kept_blocks.shape[0]
    seq = ("x", "y")
    blocks = lax.axis_size(seq)
    per_owner = heads // blocks
    rows = per_owner * BLOCK
    pair = GROUP // per_owner
    row_blocks = layer_input.shape[2] // BLOCK

    tokens = pl.BlockSpec((1, length, wide), lambda g, *_: (0, 0, g))
    col_spec = pl.BlockSpec((1, length, GROUP), lambda g, *_: (g, 0, 0))
    row_spec = pl.BlockSpec((1, GROUP, length), lambda g, *_: (g, 0, 0))
    square = pl.BlockSpec((GROUP, BLOCK, BLOCK), lambda g, *_: (g, 0, 0))
    by_head = pl.BlockSpec((GROUP, length, BLOCK), lambda g, *_: (g, 0, 0))
    flat = (1, length, width)
    head_major = (heads, length, BLOCK)
    whole = pl.BlockSpec(memory_space=pltpu.VMEM)
    anywhere = pl.BlockSpec(memory_space=pl.ANY)
    pairs = heads * length * length
    hbm, vmem = pltpu.HBM, pltpu.VMEM

    def at_start(*shape):
        return pl.BlockSpec(shape, lambda g, *_: (0,) * len(shape))

    queries, key_vectors, value_vectors = map(in_hbm, (queries, key_vectors, value_vectors))
    grad_attended, layer_input = in_hbm(grad_attended), in_hbm(layer_input)
    decay = in_hbm(log_decay[0])

    payload, col, row = call(
        "states",
        states_kernel,
        (groups,),
        [at_start(heads, length), tokens, tokens],
        [
            pl.BlockSpec((pair, rows + AUX, BLOCK), lambda g: (g, 0, 0)),
            at_start(groups, length, GROUP),
            at_start(groups, GROUP, length),
        ],
        [
            vmem((blocks, rows + AUX, BLOCK), BF16),
            vmem((groups, length, GROUP), F32),
            vmem((groups, GROUP, length), F32),
        ],
        16,
    )(decay, key_vectors, value_vectors)
    col, row = in_vmem(col), in_vmem(row)

    received = lax.all_to_all(payload, seq, 0, 0, tiled=True)

    turned = in_hbm(
        call(
            "turn",
            turn_kernel,
            (6,),
            [pl.BlockSpec((1, length, row_blocks * BLOCK // 6), lambda g: (0, 0, g))],
            pl.BlockSpec((row_blocks // 6, BLOCK, length), lambda g: (g, 0, 0)),
            hbm((row_blocks, BLOCK, length), BF16),
            32,
            (pairs * 2 * BLOCK, 2 * length * row_blocks * BLOCK * 2),
        )(layer_input)
    )

    scanned, whole_decay = call(
        "first_scan",
        first_scan_kernel,
        (),
        [whole, anywhere],
        [whole, whole],
        [vmem((blocks, rows, BLOCK), BF16), vmem((blocks, 8, BLOCK), F32)],
        8,
    )(in_vmem(received), turned)
    carried = lax.all_to_all(scanned, seq, 0, 0, tiled=True)
    carried = in_vmem(carried.reshape(heads, BLOCK, BLOCK))

    intra, scaled_q = call(
        "intra",
        intra_kernel,
        (groups,),
        [tokens, tokens, tokens, col_spec, row_spec],
        [tokens, tokens],
        [hbm(flat, F32), hbm(flat, BF16)],
        32,
        (pairs * 4 * BLOCK, 9 * length * width * 2),
    )(queries, key_vectors, value_vectors, col, row)
    intra, scaled_q = in_hbm(intra), in_hbm(scaled_q)

    attended, grad_raw, block_grad = call(
        "norm",
        norm_kernel,
        (groups,),
        [tokens, tokens, tokens, square],
        [tokens, tokens, square],
        [hbm(flat, BF16), hbm(flat, BF16), vmem((heads, BLOCK, BLOCK), BF16)],
        32,
    )(intra, scaled_q, grad_attended, carried)
    grad_raw = in_hbm(grad_raw)

    sent = lax.all_to_all(block_grad.reshape(blocks, rows, BLOCK), seq, 0, 0, tiled=True)

    grad_q, grad_q_by_head = call(
        "grad_q",
        grad_q_kernel,
        (groups,),
        [tokens, tokens, tokens, col_spec, row_spec, square],
        [tokens, by_head],
        [hbm(flat, BF16), hbm(head_major, BF16)],
        32,
        (pairs * 4 * BLOCK, 6 * length * width * 2),
    )(grad_raw, key_vectors, value_vectors, col, row, carried)
    grad_q_by_head = in_hbm(grad_q_by_head)

    scanned = call(
        "second_scan",
        second_scan_kernel,
        (),
        [whole, whole, anywhere],
        whole,
        vmem((blocks, rows, BLOCK), BF16),
        8,
    )(in_vmem(sent), in_vmem(whole_decay), grad_q_by_head)
    later = lax.all_to_all(scanned, seq, 0, 0, tiled=True)
    later = in_vmem(later.reshape(heads, BLOCK, BLOCK))

    intra_k, intra_v, scaled_k, scaled_v = call(
        "grad_kv",
        grad_kv_kernel,
        (groups,),
        [tokens, tokens, tokens, tokens, col_spec, row_spec],
        [tokens] * 4,
        [hbm(flat, BF16)] * 4,
        32,
        (pairs * 8 * BLOCK, 8 * length * width * 2),
    )(grad_raw, queries, key_vectors, value_vectors, col, row)
    intra_k, intra_v, scaled_k, scaled_v = map(in_hbm, (intra_k, intra_v, scaled_k, scaled_v))

    core = lax.axis_index("core").astype(jnp.int32).reshape(1)
    half = (kept // 2, BLOCK, BLOCK)
    grad_k, grad_v, theirs, mine = call(
        "kept",
        functools.partial(kept_kernel, heads),
        (groups,),
        [tokens, tokens, tokens, tokens, square, anywhere, anywhere],
        [tokens, tokens, at_start(*half), at_start(*half)],
        [hbm(flat, BF16), hbm(flat, BF16), vmem(half, BF16), vmem(half, BF16)],
        44,
        prefetch=2,
        scratch=[
            pltpu.VMEM((3 * heads, length, BLOCK), BF16),
            pltpu.VMEM(turned.shape, BF16),
            pltpu.SemaphoreType.DMA,
            pltpu.SemaphoreType.DMA,
        ],
    )(
        kept_blocks,
        core,
        scaled_k,
        scaled_v,
        intra_k,
        intra_v,
        later,
        grad_q_by_head,
        turned,
    )

    other = lax.ppermute(theirs, "core", [(0, 1), (1, 0)])
    chip = (mine.astype(F32) + other.astype(F32)).astype(BF16)
    parts = lax.all_to_all(chip, ("x", "y", "z"), 0, 0, tiled=True)
    tokens_all = length * lax.axis_size(("x", "y", "z", "core"))
    grad_blocks = jnp.sum(parts.astype(F32), axis=0, keepdims=True) / math.sqrt(tokens_all)
    return attended, grad_q, grad_k, grad_v, grad_blocks


def solution(mesh):
    physical = Mesh(mesh.devices.reshape(4, 4, 4, 2), ("x", "y", "z", "core"))
    seq, dp = ("x", "y"), ("z", "core")
    tokens = P(dp, seq, None)
    return jax.shard_map(
        per_device,
        mesh=physical,
        in_specs=(tokens, tokens, tokens, tokens, tokens, P(dp, None, seq), P()),
        out_specs=(tokens, tokens, tokens, tokens, P(seq + dp, None, None)),
        check_vma=False,
    )
```

```python
import functools
import math

import jax
import jax.numpy as jnp
from jax import lax
from jax.experimental import pallas as pl
from jax.experimental.pallas import tpu as pltpu
from jax.sharding import Mesh
from jax.sharding import PartitionSpec as P

BLOCK = 128
GROUP = 8
WIDE = 256
KEPT_UNROLL = 16
AUX = 16
F32 = jnp.float32
BF16 = jnp.bfloat16
MIB = 1 << 20


def dot_nt(a, b):
    return lax.dot_general(a, b, (((1,), (1,)), ((), ())), preferred_element_type=F32)


def dot_nn(a, b):
    return lax.dot_general(a, b, (((1,), (0,)), ((), ())), preferred_element_type=F32)


def dot_tn(a, b):
    return lax.dot_general(a, b, (((0,), (0,)), ((), ())), preferred_element_type=F32)


def head_slice(h):
    return slice(h * BLOCK, (h + 1) * BLOCK)


def batches(size):
    return [range(h, h + size) for h in range(0, GROUP, size)]


def group_lanes(g):
    return slice(g * GROUP * BLOCK, (g + 1) * GROUP * BLOCK)


def start_loads(pairs, groups, sems, first=0):
    loads = []
    for g in range(groups):
        at = group_lanes(g)
        copies = [
            pltpu.make_async_copy(source.at[0, :, at], buffer.at[:, at], sems.at[first + g * len(pairs) + n])
            for n, (source, buffer) in enumerate(pairs)
        ]
        for copy in copies:
            copy.start()
        loads.append(copies)
    return loads


def states_kernel(
    decay_hbm, k_hbm, v_hbm, payload_hbm, col_ref, row_ref, decay_ref, k_ref, v_ref, payload, sems
):
    length = k_ref.shape[0]
    groups = col_ref.shape[0]
    heads = groups * GROUP
    owners = GROUP // 2
    load_decay = pltpu.make_async_copy(decay_hbm, decay_ref, sems.at[3 * groups])
    load_decay.start()
    loads = start_loads([(k_hbm, k_ref), (v_hbm, v_ref)], groups, sems)
    load_decay.wait()

    decay = decay_ref[...]
    high = decay.astype(BF16).astype(F32)
    rest = decay - high
    middle = rest.astype(BF16).astype(F32)
    terms = jnp.concatenate([high, middle, rest - middle], axis=0).astype(BF16)
    t = lax.broadcasted_iota(jnp.int32, (length, length), 0)
    s = lax.broadcasted_iota(jnp.int32, (length, length), 1)
    lower = jnp.where(s <= t, 1.0, 0.0).astype(BF16)
    upper = jnp.where(t <= s, 1.0, 0.0).astype(BF16)
    cols = dot_nt(lower, terms)
    rows = dot_nn(terms, upper)
    row = rows[:heads] + rows[heads : 2 * heads] + rows[2 * heads :]
    cols = cols[:, :heads] + cols[:, heads : 2 * heads] + cols[:, 2 * heads :]
    total = cols[length - 1 : length, :]
    tails = jnp.exp(total - cols)
    whole = jnp.exp(total)
    index = lax.broadcasted_iota(jnp.int32, (AUX, BLOCK), 0)
    for g in range(groups):
        col_ref[g] = cols[:, g * GROUP : (g + 1) * GROUP]
        row_ref[g] = row[g * GROUP : (g + 1) * GROUP]
    for p in range(heads // 2):
        aux = jnp.zeros((AUX, BLOCK), F32)
        for i in range(2):
            value = jnp.broadcast_to(whole[:, 2 * p + i : 2 * p + i + 1], (AUX, BLOCK))
            first = value.astype(BF16).astype(F32)
            aux = jnp.where(index == 2 * i, first, aux)
            aux = jnp.where(index == 2 * i + 1, value - first, aux)
        payload[p, 2 * BLOCK :, :] = aux.astype(BF16)

    stores = []
    for g in range(groups):
        for copy in loads[g]:
            copy.wait()
        for batch in batches(4):
            hs = [g * GROUP + h for h in batch]
            scaled = [v_ref[:, head_slice(h)].astype(F32) * tails[:, h : h + 1] for h in hs]
            states = [dot_tn(k_ref[:, head_slice(h)], x.astype(BF16)) for h, x in zip(hs, scaled)]
            for h, state in zip(hs, states):
                payload[h // 2, head_slice(h % 2), :] = state.astype(BF16)
        at = pl.ds(g * owners, owners)
        store = pltpu.make_async_copy(payload.at[at], payload_hbm.at[at], sems.at[2 * groups + g])
        store.start()
        stores.append(store)
    for store in stores:
        store.wait()


def first_scan_kernel(x_ref, after_ref, out_ref, whole_ref):
    del after_ref
    blocks = x_ref.shape[0]
    running = [jnp.zeros((BLOCK, BLOCK), F32) for _ in range(2)]
    for j in range(blocks):
        aux = x_ref[j, 2 * BLOCK :, :].astype(F32)
        for i in range(2):
            out_ref[j, head_slice(i), :] = running[i].astype(BF16)
            whole = aux[2 * i : 2 * i + 1] + aux[2 * i + 1 : 2 * i + 2]
            whole_ref[j, i : i + 1, :] = whole
            running[i] = running[i] * whole + x_ref[j, head_slice(i), :].astype(F32)


def second_scan_kernel(x_ref, whole_ref, after_ref, out_ref):
    del after_ref
    blocks = x_ref.shape[0]
    running = [jnp.zeros((BLOCK, BLOCK), F32) for _ in range(2)]
    for j in range(blocks - 1, -1, -1):
        for i in range(2):
            out_ref[j, head_slice(i), :] = running[i].astype(BF16)
            whole = whole_ref[j, i : i + 1, :]
            running[i] = running[i] * whole + x_ref[j, head_slice(i), :].astype(F32)


def within(gap, offset):
    t = lax.broadcasted_iota(jnp.int32, gap.shape, 0)
    s = lax.broadcasted_iota(jnp.int32, gap.shape, 1) + offset
    return jnp.where(s <= t, jnp.exp(gap), 0.0)


def intra_kernel(q_ref, k_ref, v_ref, col_ref, row_ref, raw_ref, scaled_ref):
    col = col_ref[0]
    head_decay = jnp.exp(col)
    for hs in batches(2):
        parts = []
        for h in hs:
            sl = head_slice(h)
            at = slice(h, h + 1)
            scores = dot_nt(q_ref[0, :, sl], k_ref[0, :WIDE, sl])
            weights = scores * within(col[:, at] - row_ref[0, at, :WIDE], 0)
            scores = dot_nt(q_ref[0, WIDE:, sl], k_ref[0, WIDE:, sl])
            gap = col[WIDE:, at] - row_ref[0, at, WIDE:]
            parts.append((weights.astype(BF16), (scores * within(gap, 0)).astype(BF16)))
        for h, (weights, last) in zip(hs, parts):
            sl = head_slice(h)
            raw = dot_nn(weights, v_ref[0, :WIDE, sl])
            end = raw[WIDE:] + dot_nn(last, v_ref[0, WIDE:, sl])
            raw_ref[0, :WIDE, sl] = raw[:WIDE]
            raw_ref[0, WIDE:, sl] = end
            queries = q_ref[0, :, sl].astype(F32)
            scaled_ref[0, :, sl] = (queries * head_decay[:, h : h + 1]).astype(BF16)


def turn_kernel(x_ref, out_ref):
    for n in range(out_ref.shape[0]):
        out_ref[n] = x_ref[0, :, head_slice(n)].T


def norm_kernel(
    scaled_hbm,
    raw_hbm,
    g_hbm,
    carried_ref,
    attended_hbm,
    grad_raw_hbm,
    grad_hbm,
    scaled_ref,
    raw_ref,
    g_ref,
    attended_ref,
    grad_raw_ref,
    grad_ref,
    sems,
):
    groups = carried_ref.shape[0] // GROUP
    pairs = [(scaled_hbm, scaled_ref), (raw_hbm, raw_ref), (g_hbm, g_ref)]
    loads = start_loads(pairs, groups, sems)
    stores = []
    for group in range(groups):
        for copy in loads[group]:
            copy.wait()
        hs = range(group * GROUP, (group + 1) * GROUP)
        sls = [head_slice(h) for h in hs]
        raws = [dot_nn(scaled_ref[:, sl], carried_ref[h]) for h, sl in zip(hs, sls)]
        raws = [raw + raw_ref[:, sl] for raw, sl in zip(raws, sls)]
        squares = [jnp.mean(raw * raw, axis=1, keepdims=True) for raw in raws]
        shareds = [
            jnp.mean(g_ref[:, sl].astype(F32) * raw, axis=1, keepdims=True)
            for raw, sl in zip(raws, sls)
        ]
        inverses = [lax.rsqrt(square + 1e-6) for square in squares]
        grads = []
        for raw, inverse, shared, sl in zip(raws, inverses, shareds, sls):
            normed = raw * inverse
            attended_ref[:, sl] = normed.astype(BF16)
            upstream = g_ref[:, sl].astype(F32)
            grad_raw = (inverse * (upstream - normed * (shared * inverse))).astype(BF16)
            grad_raw_ref[:, sl] = grad_raw
            grads.append(grad_raw)
        for h, sl, grad_raw in zip(hs, sls, grads):
            grad_ref[h] = dot_tn(scaled_ref[:, sl], grad_raw).astype(BF16)
        at = group_lanes(group)
        heads = pl.ds(group * GROUP, GROUP)
        for n, (source, target) in enumerate(
            (
                (grad_ref.at[heads], grad_hbm.at[heads]),
                (grad_raw_ref.at[:, at], grad_raw_hbm.at[0, :, at]),
                (attended_ref.at[:, at], attended_hbm.at[0, :, at]),
            )
        ):
            store = pltpu.make_async_copy(source, target, sems.at[3 * groups + 3 * group + n])
            store.start()
            stores.append(store)
    for store in stores:
        store.wait()


def grad_q_kernel(
    grad_raw_ref,
    k_ref,
    v_ref,
    col_ref,
    row_ref,
    carried_ref,
    grad_q_ref,
    by_head_ref,
):
    col = col_ref[0]
    head_decay = jnp.exp(col)
    for hs in batches(2):
        parts = []
        for h in hs:
            sl = head_slice(h)
            at = slice(h, h + 1)
            scores = dot_nt(grad_raw_ref[0, :, sl], v_ref[0, :WIDE, sl])
            dscores = scores * within(col[:, at] - row_ref[0, at, :WIDE], 0)
            scores = dot_nt(grad_raw_ref[0, WIDE:, sl], v_ref[0, WIDE:, sl])
            gap = col[WIDE:, at] - row_ref[0, at, WIDE:]
            parts.append((dscores.astype(BF16), (scores * within(gap, 0)).astype(BF16)))
        for h, (dscores, last) in zip(hs, parts):
            sl = head_slice(h)
            carried = dot_nt(grad_raw_ref[0, :, sl], carried_ref[h])
            grad_q = dot_nn(dscores, k_ref[0, :WIDE, sl]) + head_decay[:, h : h + 1] * carried
            end = grad_q[WIDE:] + dot_nn(last, k_ref[0, WIDE:, sl])
            for cut, part in ((slice(0, WIDE), grad_q[:WIDE]), (slice(WIDE, None), end)):
                part = part.astype(BF16)
                grad_q_ref[0, cut, sl] = part
                by_head_ref[h, cut, :] = part


def grad_kv_kernel(
    grad_raw_ref,
    q_ref,
    k_ref,
    v_ref,
    col_ref,
    row_ref,
    grad_k_ref,
    grad_v_ref,
    scaled_k_ref,
    scaled_v_ref,
):
    length = k_ref.shape[1]
    col = col_ref[0]
    tail = jnp.exp(col[length - 1 : length, :] - col)
    split = length - WIDE

    def turned_within(h, rows, start, stop):
        gap = row_ref[0, h : h + 1, start:stop] - col[:rows, h : h + 1]
        s = lax.broadcasted_iota(jnp.int32, gap.shape, 0)
        t = lax.broadcasted_iota(jnp.int32, gap.shape, 1) + start
        return jnp.where(s <= t, jnp.exp(gap), 0.0)

    for hs in batches(2):
        parts = []
        for h in hs:
            sl = head_slice(h)
            near = turned_within(h, length, split, length)
            first = turned_within(h, split, 0, split)
            parts.append(
                [
                    (dot_nt(k_ref[0, :, sl], q_ref[0, split:, sl]) * near).astype(BF16),
                    (dot_nt(v_ref[0, :, sl], grad_raw_ref[0, split:, sl]) * near).astype(BF16),
                    (dot_nt(k_ref[0, :split, sl], q_ref[0, :split, sl]) * first).astype(BF16),
                    (dot_nt(v_ref[0, :split, sl], grad_raw_ref[0, :split, sl]) * first).astype(BF16),
                ]
            )
        for h, (weights, dscores, first_weights, first_dscores) in zip(hs, parts):
            sl = head_slice(h)
            grad_k = dot_nn(dscores, q_ref[0, split:, sl])
            grad_v = dot_nn(weights, grad_raw_ref[0, split:, sl])
            first_k = grad_k[:split] + dot_nn(first_dscores, q_ref[0, :split, sl])
            first_v = grad_v[:split] + dot_nn(first_weights, grad_raw_ref[0, :split, sl])
            grad_k_ref[0, :split, sl] = first_k.astype(BF16)
            grad_k_ref[0, split:, sl] = grad_k[split:].astype(BF16)
            grad_v_ref[0, :split, sl] = first_v.astype(BF16)
            grad_v_ref[0, split:, sl] = grad_v[split:].astype(BF16)
            factor = tail[:, h : h + 1]
            scaled_k_ref[0, :, sl] = (k_ref[0, :, sl].astype(F32) * factor).astype(BF16)
            scaled_v_ref[0, :, sl] = (v_ref[0, :, sl].astype(F32) * factor).astype(BF16)


def kept_products(kept_ref, turned, stack, out_ref, parity):
    per_row = stack.shape[0]

    def body(i, carry):
        number = kept_ref[2 * i + parity]
        left = turned[number // per_row]
        right = stack[lax.rem(number, per_row)]
        out_ref[i] = dot_nn(left, right).astype(BF16)
        return carry

    lax.fori_loop(0, out_ref.shape[0], body, 0, unroll=KEPT_UNROLL)


def theirs_kernel(
    kept_ref,
    core_ref,
    scaled_k_hbm,
    scaled_v_hbm,
    intra_k_hbm,
    intra_v_hbm,
    later_ref,
    by_head_hbm,
    turned_hbm,
    grad_k_hbm,
    grad_v_hbm,
    theirs_ref,
    stack,
    turned,
    scaled_k_ref,
    scaled_v_ref,
    intra_k_ref,
    intra_v_ref,
    grad_k_ref,
    grad_v_ref,
    sems,
):
    heads = later_ref.shape[0]
    groups = heads // GROUP
    pairs = [
        (scaled_v_hbm, scaled_v_ref),
        (scaled_k_hbm, scaled_k_ref),
        (intra_k_hbm, intra_k_ref),
        (intra_v_hbm, intra_v_ref),
    ]
    loads = start_loads(pairs, groups, sems)
    others = (
        pltpu.make_async_copy(by_head_hbm, stack.at[pl.ds(0, heads)], sems.at[6 * groups]),
        pltpu.make_async_copy(turned_hbm, turned, sems.at[6 * groups + 1]),
    )
    for copy in others:
        copy.start()
    stores = []
    for group in range(groups):
        for copy in loads[group]:
            copy.wait()
        for batch in batches(4):
            hs = [group * GROUP + h for h in batch]
            sls = [head_slice(h) for h in hs]
            grads_k = [dot_nt(scaled_v_ref[:, sl], later_ref[h]) for h, sl in zip(hs, sls)]
            grads_v = [dot_nn(scaled_k_ref[:, sl], later_ref[h]) for h, sl in zip(hs, sls)]
            for h, sl, grad_k, grad_v in zip(hs, sls, grads_k, grads_v):
                grad_k = (intra_k_ref[:, sl].astype(F32) + grad_k).astype(BF16)
                grad_v = (intra_v_ref[:, sl].astype(F32) + grad_v).astype(BF16)
                grad_k_ref[:, sl] = grad_k
                grad_v_ref[:, sl] = grad_v
                stack[heads + h] = grad_k
                stack[2 * heads + h] = grad_v
        at = group_lanes(group)
        for n, (source, target) in enumerate(((grad_k_ref, grad_k_hbm), (grad_v_ref, grad_v_hbm))):
            store = pltpu.make_async_copy(
                source.at[:, at], target.at[0, :, at], sems.at[4 * groups + 2 * group + n]
            )
            store.start()
            stores.append(store)
    for copy in others:
        copy.wait()
    kept_products(kept_ref, turned, stack, theirs_ref, 1 - core_ref[0])
    for store in stores:
        store.wait()


def mine_kernel(kept_ref, core_ref, stack, turned, mine_ref):
    kept_products(kept_ref, turned, stack, mine_ref, core_ref[0])


def in_hbm(x):
    return pltpu.with_memory_space_constraint(x, pltpu.HBM)


def in_vmem(x):
    return pltpu.with_memory_space_constraint(x, pltpu.VMEM)


def call(name, kernel, grid, in_specs, out_specs, out_shape, mib, work=None, prefetch=0, scratch=()):
    estimate = None
    if work is not None:
        estimate = pl.CostEstimate(flops=work[0], bytes_accessed=work[1], transcendentals=0)
    return pl.pallas_call(
        kernel,
        grid_spec=pltpu.PrefetchScalarGridSpec(
            num_scalar_prefetch=prefetch,
            grid=grid,
            in_specs=in_specs,
            out_specs=out_specs,
            scratch_shapes=scratch,
        ),
        out_shape=out_shape,
        compiler_params=pltpu.CompilerParams(
            dimension_semantics=("arbitrary",) * len(grid), vmem_limit_bytes=mib * MIB
        ),
        cost_estimate=estimate,
        name=name,
    )


def per_device(
    layer_input, queries, key_vectors, value_vectors, grad_attended, log_decay, kept_blocks
):
    heads = log_decay.shape[1]
    length = queries.shape[1]
    width = queries.shape[2]
    groups = heads // GROUP
    wide = GROUP * BLOCK
    kept = kept_blocks.shape[0]
    seq = ("x", "y")
    blocks = lax.axis_size(seq)
    per_owner = heads // blocks
    rows = per_owner * BLOCK
    pair = GROUP // per_owner
    row_blocks = layer_input.shape[2] // BLOCK

    tokens = pl.BlockSpec((1, length, wide), lambda g, *_: (0, 0, g))
    col_spec = pl.BlockSpec((1, length, GROUP), lambda g, *_: (g, 0, 0))
    row_spec = pl.BlockSpec((1, GROUP, length), lambda g, *_: (g, 0, 0))
    square = pl.BlockSpec((GROUP, BLOCK, BLOCK), lambda g, *_: (g, 0, 0))
    by_head = pl.BlockSpec((GROUP, length, BLOCK), lambda g, *_: (g, 0, 0))
    flat = (1, length, width)
    head_major = (heads, length, BLOCK)
    whole = pl.BlockSpec(memory_space=pltpu.VMEM)
    anywhere = pl.BlockSpec(memory_space=pl.ANY)
    pairs = heads * length * length
    hbm, vmem = pltpu.HBM, pltpu.VMEM

    def at_start(*shape):
        return pl.BlockSpec(shape, lambda g, *_: (0,) * len(shape))

    queries, key_vectors, value_vectors = map(in_hbm, (queries, key_vectors, value_vectors))
    grad_attended, layer_input = in_hbm(grad_attended), in_hbm(layer_input)
    decay = in_hbm(log_decay[0])

    tall = (length, width)
    payload, col, row = call(
        "states",
        states_kernel,
        (),
        [anywhere, anywhere, anywhere],
        [anywhere, whole, whole],
        [
            hbm((blocks, rows + AUX, BLOCK), BF16),
            vmem((groups, length, GROUP), F32),
            vmem((groups, GROUP, length), F32),
        ],
        24,
        scratch=[
            pltpu.VMEM((heads, length), F32),
            pltpu.VMEM(tall, BF16),
            pltpu.VMEM(tall, BF16),
            pltpu.VMEM((blocks, rows + AUX, BLOCK), BF16),
            pltpu.SemaphoreType.DMA((3 * groups + 1,)),
        ],
    )(decay, key_vectors, value_vectors)
    col, row = in_vmem(col), in_vmem(row)

    received = lax.all_to_all(payload, seq, 0, 0, tiled=True)

    turned = in_hbm(
        call(
            "turn",
            turn_kernel,
            (6,),
            [pl.BlockSpec((1, length, row_blocks * BLOCK // 6), lambda g: (0, 0, g))],
            pl.BlockSpec((row_blocks // 6, BLOCK, length), lambda g: (g, 0, 0)),
            hbm((row_blocks, BLOCK, length), BF16),
            32,
            (pairs * 2 * BLOCK, 2 * length * row_blocks * BLOCK * 2),
        )(layer_input)
    )

    scanned, whole_decay = call(
        "first_scan",
        first_scan_kernel,
        (),
        [whole, anywhere],
        [whole, whole],
        [hbm((blocks, rows, BLOCK), BF16), vmem((blocks, 8, BLOCK), F32)],
        8,
    )(in_vmem(received), turned)
    carried = lax.all_to_all(scanned, seq, 0, 0, tiled=True)
    carried = in_vmem(carried.reshape(heads, BLOCK, BLOCK))

    intra, scaled_q = call(
        "intra",
        intra_kernel,
        (groups,),
        [tokens, tokens, tokens, col_spec, row_spec],
        [tokens, tokens],
        [hbm(flat, F32), hbm(flat, BF16)],
        32,
        (pairs * 4 * BLOCK, 9 * length * width * 2),
    )(queries, key_vectors, value_vectors, col, row)
    intra, scaled_q = in_hbm(intra), in_hbm(scaled_q)

    attended, grad_raw, block_grad = call(
        "norm",
        norm_kernel,
        (),
        [anywhere, anywhere, anywhere, whole],
        [anywhere, anywhere, anywhere],
        [hbm(flat, BF16), hbm(flat, BF16), hbm((heads, BLOCK, BLOCK), BF16)],
        32,
        scratch=[
            pltpu.VMEM(tall, BF16),
            pltpu.VMEM(tall, F32),
            pltpu.VMEM(tall, BF16),
            pltpu.VMEM(tall, BF16),
            pltpu.VMEM(tall, BF16),
            pltpu.VMEM((heads, BLOCK, BLOCK), BF16),
            pltpu.SemaphoreType.DMA((6 * groups,)),
        ],
    )(scaled_q, intra, grad_attended, carried)
    grad_raw = in_hbm(grad_raw)

    sent = lax.all_to_all(block_grad.reshape(blocks, rows, BLOCK), seq, 0, 0, tiled=True)

    grad_q, grad_q_by_head = call(
        "grad_q",
        grad_q_kernel,
        (groups,),
        [tokens, tokens, tokens, col_spec, row_spec, square],
        [tokens, by_head],
        [hbm(flat, BF16), hbm(head_major, BF16)],
        32,
        (pairs * 4 * BLOCK, 6 * length * width * 2),
    )(grad_raw, key_vectors, value_vectors, col, row, carried)
    grad_q_by_head = in_hbm(grad_q_by_head)

    scanned = call(
        "second_scan",
        second_scan_kernel,
        (),
        [whole, whole, anywhere],
        whole,
        hbm((blocks, rows, BLOCK), BF16),
        8,
    )(in_vmem(sent), in_vmem(whole_decay), grad_q_by_head)
    later = lax.all_to_all(scanned, seq, 0, 0, tiled=True)
    later = in_vmem(later.reshape(heads, BLOCK, BLOCK))

    intra_k, intra_v, scaled_k, scaled_v = call(
        "grad_kv",
        grad_kv_kernel,
        (groups,),
        [tokens, tokens, tokens, tokens, col_spec, row_spec],
        [tokens] * 4,
        [hbm(flat, BF16)] * 4,
        32,
        (pairs * 8 * BLOCK, 8 * length * width * 2),
    )(grad_raw, queries, key_vectors, value_vectors, col, row)
    intra_k, intra_v, scaled_k, scaled_v = map(in_hbm, (intra_k, intra_v, scaled_k, scaled_v))

    core = lax.axis_index("core").astype(jnp.int32).reshape(1)
    half = (kept // 2, BLOCK, BLOCK)
    stack_shape = (3 * heads, length, BLOCK)
    grad_k, grad_v, theirs, stack, turned = call(
        "theirs",
        theirs_kernel,
        (),
        [anywhere, anywhere, anywhere, anywhere, whole, anywhere, anywhere],
        [anywhere, anywhere, whole, whole, whole],
        [
            hbm(flat, BF16),
            hbm(flat, BF16),
            vmem(half, BF16),
            vmem(stack_shape, BF16),
            vmem(turned.shape, BF16),
        ],
        40,
        prefetch=2,
        scratch=[
            pltpu.VMEM(tall, BF16),
            pltpu.VMEM(tall, BF16),
            pltpu.VMEM(tall, BF16),
            pltpu.VMEM(tall, BF16),
            pltpu.VMEM(tall, BF16),
            pltpu.VMEM(tall, BF16),
            pltpu.SemaphoreType.DMA((6 * groups + 2,)),
        ],
    )(
        kept_blocks,
        core,
        scaled_k,
        scaled_v,
        intra_k,
        intra_v,
        later,
        grad_q_by_head,
        turned,
    )
    mine = call(
        "mine",
        mine_kernel,
        (),
        [whole, whole],
        whole,
        vmem(half, BF16),
        20,
        (2 * kept * length * BLOCK * BLOCK, kept * BLOCK * BLOCK * 2),
        prefetch=2,
    )(kept_blocks, core, in_vmem(stack), in_vmem(turned))

    other = lax.ppermute(theirs, "core", [(0, 1), (1, 0)])
    chip = (mine.astype(F32) + other.astype(F32)).astype(BF16)
    parts = lax.all_to_all(chip, ("x", "y", "z"), 0, 0, tiled=True)
    tokens_all = length * lax.axis_size(("x", "y", "z", "core"))
    grad_blocks = jnp.sum(parts.astype(F32), axis=0, keepdims=True) / math.sqrt(tokens_all)
    return attended, grad_q, grad_k, grad_v, grad_blocks


def solution(mesh):
    physical = Mesh(mesh.devices.reshape(4, 4, 4, 2), ("x", "y", "z", "core"))
    seq, dp = ("x", "y"), ("z", "core")
    tokens = P(dp, seq, None)
    return jax.shard_map(
        per_device,
        mesh=physical,
        in_specs=(tokens, tokens, tokens, tokens, tokens, P(dp, None, seq), P()),
        out_specs=(tokens, tokens, tokens, tokens, P(seq + dp, None, None)),
        check_vma=False,
    )
```
